32 devices in a mesh: seq: 16 (over z, x, core), head: 2 (over y).
Axes of the slice: x: 2, y: 2, z: 4, core: 2. Of those that a mesh axis runs over, the one named last changes fastest.
Arguments:
- queries: bfloat16 [2048, 8192], P('seq', 'head'), may hold values from -14 to 14, as said below
- key_tokens: bfloat16 [2048, 1024], P(('seq', 'head')), may hold values from -6 to 6, as said below
- value_tokens: bfloat16 [2048, 1024], P(('seq', 'head')), may hold values from -6 to 6
- key_scales: bfloat16 [32, 8], P('seq', 'head'), may hold values from 0.25 to 2.5
- value_scales: bfloat16 [32, 8], P('seq', 'head'), may hold values from 0.25 to 2.5
- value_means: float32 [1024], P('head'), may hold values from -4 to 4
- doc_lengths: int32 [64], replicated, may hold values from 1 to 1280, 2048 in all
Outputs:
- attended: bfloat16 [2048, 8192], P('seq', 'head')
The draws below stay inside these ranges and needn't reach their ends.
Inputs may be any that keep to these rules, and one draw needn't show every extreme that they name: `doc_lengths`: positive lengths of the documents in order; they sum to 2048, and the longest has exactly 1280 tokens. `queries`: finite values. `key_tokens`: finite values.
All inputs are finite; a program needn't handle non-finite values.
Results may differ from the reference program's by a relative error of at most 0.002.
Values may be sent and summed in bfloat16 or wider, within the bound.
A program may use at most 64 MiB of HBM per device.

```python
import math
import jax
import jax.numpy as jnp
import numpy as np
from jax import lax

QH = 64
KVH = 8
HD = 128
BLK = 64
DOCS = 64
TOKENS = 2048
MOST = 1280


def shared_keys(key):
    base_key = jax.random.fold_in(key, 11)
    raw_values = jnp.clip(jax.random.normal(base_key, (TOKENS, KVH, HD), jnp.float32), -6.0, 6.0)
    return raw_values


def draw_key_tokens(key, part):
    return shared_keys(key).reshape(TOKENS, KVH * HD).astype(jnp.bfloat16)


def draw_queries(key, part):
    group_size = QH // KVH
    base_key = jax.random.fold_in(key, 23)
    raw_values = jnp.clip(jax.random.normal(base_key, (TOKENS, KVH, group_size, HD), jnp.float32), -6.0, 6.0)
    return raw_values.reshape(TOKENS, QH * HD).astype(jnp.bfloat16)


def level_of(stream_key, shape, shards, least, top_value):
    loudness, own = 1.0, jax.random.fold_in(stream_key, 6)
    for dim, blocks in shards:
        heights = jnp.exp(jax.random.uniform(jax.random.fold_in(own, dim), (blocks,), jnp.float32, least / len(shards), top_value / len(shards)))
        loudness = loudness * jnp.repeat(heights, shape[dim] // blocks).reshape([-1 if axis == dim else 1 for axis in range(len(shape))])
    return loudness


def profile(number_of, total, reach, lean):
    portions = [(1 << 20) // math.isqrt(grade ** lean) + 1 for grade in range(2, number_of + 1)]
    rest, given = total - reach - (number_of - 1), [1] * (number_of - 1)
    while rest > 0:
        movable = [i for i in range(number_of - 1) if given[i] < reach]
        mass, left = sum([portions[i] for i in movable]), rest
        for i in movable:
            more = min(reach - given[i], max(1, left * portions[i] // mass), rest)
            given[i] = given[i] + more
            rest = rest - more
    return np.array([reach] + given)


def ragged(stream_key, count, total, reach, slope):
    if count == 2:
        one = jax.random.randint(stream_key, (), max(1, total - reach), min(reach, total - 1) + 1)
        return jnp.stack([one, total - one])
    lengths = jnp.asarray(profile(count, total, reach, slope), jnp.int32)
    pairs = (count - 1) // 2
    giver, taker = lengths[1:1 + 2 * pairs:2], lengths[2:2 + 2 * pairs:2]
    margin = jnp.minimum(giver - 1, reach - taker)
    shifted = jax.random.randint(jax.random.fold_in(stream_key, 1), (pairs,), 0, 1 << 20) % (margin + 1)
    lengths = lengths.at[1:1 + 2 * pairs:2].set(giver - shifted).at[2:2 + 2 * pairs:2].set(taker + shifted)
    return lengths[jax.random.permutation(jax.random.fold_in(stream_key, 2), count)]


def centred(own_key, shape, width, most, pieces=(), kind=jnp.bfloat16):
    loudness = level_of(own_key, shape, pieces, -0.22, 0.18) if pieces else 1.0
    values = jax.random.normal(own_key, shape, jnp.float32) * width * loudness
    return jnp.minimum(jnp.maximum(values, -most), most).astype(kind)


def setup_inputs(seed: int = 0) -> dict:
    splits = jax.random.split(jax.random.key(seed), 8)
    return {
        "queries": draw_queries(jax.random.fold_in(splits[7], 71), 0),
        "key_tokens": draw_key_tokens(jax.random.fold_in(splits[7], 71), 0),
        "value_tokens": centred(splits[2], (TOKENS, KVH * HD), 1.0, 6.0, ((0, 32),)),
        "key_scales": jnp.clip(jnp.exp(math.log(2.5) - 2.3025851 * jax.random.uniform(splits[3], (TOKENS // BLK, KVH), jnp.float32) ** level_of(splits[3], (TOKENS // BLK, KVH), ((0, 16), (1, 2)), -0.2, 0.2)), 0.25, 2.5).astype(jnp.bfloat16),
        "value_scales": jnp.clip(jnp.exp(math.log(2.5) - 2.3025851 * jax.random.uniform(splits[4], (TOKENS // BLK, KVH), jnp.float32) ** level_of(splits[4], (TOKENS // BLK, KVH), ((0, 16), (1, 2)), -0.2, 0.2)), 0.25, 2.5).astype(jnp.bfloat16),
        "value_means": centred(splits[5], (KVH * HD,), 1.0, 4.0, ((0, 2),), jnp.float32),
        "doc_lengths": ragged(splits[6], DOCS, TOKENS, MOST, 1).astype(jnp.int32),
    }


NEG = -1e+30

def reference(queries, key_tokens, value_tokens, key_scales, value_scales, value_means, doc_lengths):
    token_count = queries.shape[0]
    group_size = QH // KVH
    inv_scale = 1.0 / math.sqrt(HD)
    starts = jnp.cumsum(doc_lengths) - doc_lengths
    positions = jnp.arange(token_count, dtype=jnp.int32)
    docs = lax.optimization_barrier(jnp.sum((starts[None, :] <= positions[:, None]).astype(jnp.int32), axis=1)) - 1
    query_block = math.gcd(token_count, 128)
    window = min(MOST + query_block, token_count)
    key_heads = key_tokens.reshape(token_count, KVH, HD)
    value_heads = value_tokens.reshape(token_count, KVH, HD)
    key_scale_rows = jnp.repeat(key_scales.astype(jnp.float32), BLK, axis=0)
    value_scale_rows = jnp.repeat(value_scales.astype(jnp.float32), BLK, axis=0)
    query_heads = queries.reshape(token_count, KVH, group_size, HD)
    mean_rows = value_means.reshape(KVH, 1, 1, HD)

    def one_block(first_query):
        first_key = jnp.clip(first_query + query_block - window, 0, token_count - window).astype(jnp.int32)
        query_tile = lax.dynamic_slice_in_dim(query_heads, first_query, query_block, 0).astype(jnp.float32)
        key_tile = lax.dynamic_slice_in_dim(key_heads, first_key, window, 0).astype(jnp.float32)
        value_tile = lax.dynamic_slice_in_dim(value_heads, first_key, window, 0).astype(jnp.float32)
        key_scale_tile = lax.dynamic_slice_in_dim(key_scale_rows, first_key, window, 0)
        value_scale_tile = lax.dynamic_slice_in_dim(value_scale_rows, first_key, window, 0)
        query_pos = first_query + jnp.arange(query_block, dtype=jnp.int32)
        key_pos = first_key + jnp.arange(window, dtype=jnp.int32)
        query_doc = lax.dynamic_slice_in_dim(docs, first_query, query_block, 0)
        key_doc = lax.dynamic_slice_in_dim(docs, first_key, window, 0)
        allowed = (key_doc[None, :] == query_doc[:, None]) & (key_pos[None, :] <= query_pos[:, None])
        scores = jnp.einsum('rkgd,nkd->kgrn', query_tile, key_tile)
        scores = scores * (key_scale_tile.T * inv_scale)[:, None, None, :]
        scores = jnp.where(allowed[None, None], scores, NEG)
        peak = lax.optimization_barrier(jnp.max(scores, axis=-1))
        weights = jnp.where(allowed[None, None], jnp.exp(scores - peak[..., None]), 0.0)
        total = lax.optimization_barrier(jnp.sum(weights, axis=-1))
        scaled = (weights * value_scale_tile.T[:, None, None, :]).astype(jnp.bfloat16)
        scaled = lax.optimization_barrier(scaled).astype(jnp.float32)
        mixture = jnp.einsum('kgrn,nkd->kgrd', scaled, value_tile)
        result = mixture / total[..., None] + mean_rows
        return result.transpose(2, 0, 1, 3).reshape(query_block, QH * HD).astype(jnp.bfloat16)
    firsts = jnp.arange(token_count // query_block, dtype=jnp.int32) * query_block
    blocks_out = lax.map(one_block, firsts)
    return blocks_out.reshape(token_count, QH * HD)
```

```python
import functools
import math

import jax
import jax.numpy as jnp
from jax import lax
from jax.experimental import pallas as pl
from jax.experimental.pallas import tpu as pltpu
from jax.sharding import PartitionSpec as P

QH = 64
KVH = 8
HD = 128
BLK = 64
G = QH // KVH
NEG = -1e30
MESH = pl.DeviceIdType.MESH
SCALE = math.log2(math.e) / math.sqrt(HD)


def kernel(
    dims,
    doc_ref,
    q_hbm,
    k_hbm,
    v_hbm,
    ks_ref,
    vs_ref,
    mean_ref,
    out_hbm,
    buf,
    q_vm,
    qt,
    acc,
    m_ref,
    l_ref,
    out_vm,
    bias,
    lo_ref,
    local_sem,
    out_sem,
    head_send,
    head_recv,
    send,
    recv,
):
    planes, nh, rows, hk, toks, reach = dims
    cols = hk * HD
    s = lax.axis_index("seq")
    h = lax.axis_index("head")
    z, x, c = s // 4, (s // 2) % 2, s % 2
    g = s // 2
    zdst, xdst, cdst = s + 4, s + 2 - 4 * x, s + 1 - 2 * c

    barrier = pltpu.get_barrier_semaphore()

    def greet(seq, head):
        pl.semaphore_signal(barrier, inc=1, device_id=(seq, head), device_id_type=MESH)

    for step in range(1, nh):
        greet(s, (h + step) % nh)
    greet(xdst, h)
    greet(cdst, h)

    @pl.when(z > 0)
    def _():
        greet(s - 4, h)

    @pl.when(z < planes - 1)
    def _():
        greet(s + 4, h)

    q_copy = pltpu.make_async_copy(q_hbm, q_vm, local_sem.at[0])
    q_copy.start()
    own_cols = pl.ds(pl.multiple_of(h * cols, HD), cols)
    locals_ = []
    for piece, hbm in enumerate((k_hbm, v_hbm)):
        dst = buf.at[s, pl.ds(pl.multiple_of(piece * rows + h * toks, 16), toks)]
        locals_.append(pltpu.make_async_copy(hbm.at[:, own_cols], dst, local_sem.at[1 + piece]))
        locals_[-1].start()

    pl.semaphore_wait(
        barrier,
        nh + 1 + jnp.where(z > 0, 1, 0) + jnp.where(z < planes - 1, 1, 0),
    )

    head_copies = []
    for piece, hbm in enumerate((k_hbm, v_hbm)):
        for step in range(1, nh):
            peer = (h + step) % nh
            peer_cols = pl.ds(pl.multiple_of(peer * cols, HD), cols)
            dst = buf.at[s, pl.ds(pl.multiple_of(piece * rows + h * toks, 16), toks)]
            head_copies.append(
                pltpu.make_async_remote_copy(
                    src_ref=hbm.at[:, peer_cols],
                    dst_ref=dst,
                    send_sem=head_send.at[piece, step - 1],
                    recv_sem=head_recv.at[piece, step - 1],
                    device_id=(s, peer),
                    device_id_type=MESH,
                )
            )
            head_copies[-1].start()

    per = rows // BLK
    pieces = []
    for ref in (ks_ref, vs_ref):
        sc = ref[...].astype(jnp.float32)
        pieces.append(
            jnp.concatenate(
                [jnp.broadcast_to(sc[:, i : i + 1], (per, HD)) for i in range(hk)], axis=1
            )
        )
    pieces.append(jnp.zeros((16 - 2 * per, cols), jnp.float32))
    buf[s, 2 * rows :, :] = jnp.concatenate(pieces, axis=0).astype(jnp.bfloat16)

    def part(slot, p):
        if p == 0:
            return buf.at[slot, pl.ds(0, rows)]
        return buf.at[slot, pl.ds(rows, rows + 16)]

    def copy(kind, slot, p, dst):
        return pltpu.make_async_remote_copy(
            src_ref=part(slot, p),
            dst_ref=part(slot, p),
            send_sem=send.at[kind, slot, p],
            recv_sem=recv.at[slot, p],
            device_id=(dst, h),
            device_id_type=MESH,
        )

    def need(g0, at):
        return (g0 >= 0) & (g0 <= at) & (g0 >= at - reach)

    def routes(g0, chain):
        out = [(2, need(g0, g), cdst)]
        if chain:
            up = (z + 1 < planes) & (g0 >= 0) & (g0 >= 2 * (z + 1) - reach)
            across = need(g0, 2 * z + 1 - x)
            out = [(0, up, zdst), (1, across, xdst)] + out
        return out

    def forward(g0, chain, p):
        for kind, cond, dst in routes(g0, chain):

            @pl.when(cond)
            def _(kind=kind, dst=dst):
                copy(kind, g0 * 2 + c, p, dst).start()

    def drain(g0, chain):
        for kind, cond, dst in routes(g0, chain):

            @pl.when(cond)
            def _(kind=kind, dst=dst):
                for p in range(2):
                    copy(kind, g0 * 2 + c, p, dst).wait_send()

    def arrive(slot, p):
        copy(2, slot, p, cdst).wait_recv()

    for piece in range(2):
        locals_[piece].wait()
        for step in range(1, nh):
            head_copies[piece * (nh - 1) + step - 1].wait_recv()
        forward(g, True, piece)

    pos = s * rows + lax.broadcasted_iota(jnp.int32, (1, rows), 1)
    start = jnp.int32(0)
    low = jnp.zeros((1, rows), jnp.int32)
    for j in range(doc_ref.shape[0]):
        low = jnp.where(pos >= start, start, low)
        start = start + doc_ref[j]
    lo_ref[...] = low
    m_ref[...] = jnp.full(m_ref.shape, NEG, jnp.float32)
    l_ref[...] = jnp.zeros(l_ref.shape, jnp.float32)
    acc[...] = jnp.zeros(acc.shape, jnp.float32)
    q_copy.wait()
    for i in range(hk):
        for j in range(G):
            tile = q_vm[:, (i * G + j) * HD : (i * G + j + 1) * HD]
            qt[i, :, j * rows : (j + 1) * rows] = tile.T

    keys = 2 * rows
    blocks = keys // BLK
    wide = 2 * rows

    def compute(g0):
        key_pos = g0 * keys + lax.broadcasted_iota(jnp.int32, (keys, rows), 0)
        query_pos = s * rows + lax.broadcasted_iota(jnp.int32, (keys, rows), 1)
        ok = (key_pos >= lo_ref[...]) & (key_pos <= query_pos)
        bias[...] = jnp.where(ok, 0.0, NEG)

        def one_head(i, carry):
            lanes = pl.ds(pl.multiple_of(i * HD, HD), HD)
            k = buf[pl.ds(2 * g0, 2), 0:rows, lanes].reshape(keys, HD)
            v = buf[pl.ds(2 * g0, 2), rows : 2 * rows, lanes].reshape(keys, HD)
            vt = v.T
            sc = buf[pl.ds(2 * g0, 2), 2 * rows : 2 * rows + 16, lanes].astype(jnp.float32)
            ks = sc[:, 0:per].reshape(blocks, 1, HD) * SCALE
            vs = sc[:, per : 2 * per].reshape(blocks, 1, HD)
            ks = jnp.concatenate([ks, ks], axis=2)
            vs = jnp.concatenate([vs, vs], axis=2)
            mask = bias[...]
            mask = jnp.concatenate([mask, mask], axis=1)
            for j in range(G * rows // wide):
                at = slice(j * wide, (j + 1) * wide)
                sco = jnp.dot(k, qt[i, :, at], preferred_element_type=jnp.float32)
                sco = (sco.reshape(blocks, BLK, wide) * ks).reshape(keys, wide) + mask
                old = m_ref[i, :, at]
                new = jnp.maximum(old, jnp.max(sco, axis=0, keepdims=True))
                w = jnp.exp2(sco - new)
                fac = jnp.exp2(old - new)
                m_ref[i, :, at] = new
                l_ref[i, :, at] = l_ref[i, :, at] * fac + jnp.sum(w, axis=0, keepdims=True)
                wb = (w.reshape(blocks, BLK, wide) * vs).reshape(keys, wide).astype(jnp.bfloat16)
                acc[i, :, at] = acc[i, :, at] * fac + jnp.dot(
                    vt, wb, preferred_element_type=jnp.float32
                )
            return carry

        lax.fori_loop(0, hk, one_head, 0)

    def sibling(g0):
        for p in range(2):
            arrive(g0 * 2 + 1 - c, p)

    def across_block(dz):
        g0 = 2 * (z - dz) + 1 - x

        @pl.when(need(g0, g))
        def _():
            for p in range(2):
                arrive(g0 * 2 + c, p)
                forward(g0, False, p)
            sibling(g0)
            compute(g0)

    sibling(g)
    compute(g)
    last = (reach + 1) // 2

    def one_plane(dz, carry):
        g0 = 2 * (z - dz) + x

        @pl.when((g0 >= 0) & (g0 >= 2 * z - reach))
        def _():
            for p in range(2):
                arrive(g0 * 2 + c, p)
                forward(g0, True, p)

        across_block(dz - 1)

        @pl.when(need(g0, g))
        def _():
            sibling(g0)
            compute(g0)

        return carry

    lax.fori_loop(1, last + 1, one_plane, 0)
    across_block(last)

    outs = []
    for i in range(hk):
        for j in range(G):
            at = slice(j * rows, (j + 1) * rows)
            o = acc[i, :, at] * (1.0 / l_ref[i, :, at])
            o = o.T + mean_ref[:, i * HD : (i + 1) * HD]
            out_vm[:, (i * G + j) * HD : (i * G + j + 1) * HD] = o.astype(jnp.bfloat16)
        span = pl.ds(i * G * HD, G * HD)
        outs.append(pltpu.make_async_copy(out_vm.at[:, span], out_hbm.at[:, span], out_sem.at[i]))
        outs[-1].start()

    for one in head_copies:
        one.wait_send()

    def settle(dz, carry):
        g0 = 2 * (z - dz) + x

        @pl.when((dz == 0) | (g0 >= 0) & (g0 >= 2 * z - reach))
        def _():
            drain(g0, True)

        g1 = 2 * (z - dz) + 1 - x

        @pl.when(need(g1, g))
        def _():
            drain(g1, False)

        return carry

    lax.fori_loop(0, last + 1, settle, 0)
    for one in outs:
        one.wait()


def shards(queries, key_tokens, value_tokens, key_scales, value_scales, value_means, doc_lengths, nseq, nh):
    rows, width = queries.shape
    toks = key_tokens.shape[0]
    hk = width // (G * HD)
    cols = hk * HD
    most = nseq * rows * 5 // 8
    window = (most - 1 + rows - 1) // rows
    reach = (window + 1) // 2
    dims = (nseq // 4, nh, rows, hk, toks, reach)
    anyspace = pl.BlockSpec(memory_space=pl.ANY)
    vmem = pl.BlockSpec(memory_space=pltpu.VMEM)
    smem = pl.BlockSpec(memory_space=pltpu.SMEM)
    dma = pltpu.SemaphoreType.DMA
    return pl.pallas_call(
        functools.partial(kernel, dims),
        out_shape=jax.ShapeDtypeStruct((rows, width), jnp.bfloat16),
        in_specs=[smem, anyspace, anyspace, anyspace, vmem, vmem, vmem],
        out_specs=anyspace,
        scratch_shapes=[
            pltpu.VMEM((nseq, 2 * rows + 16, cols), jnp.bfloat16),
            pltpu.VMEM((rows, width), jnp.bfloat16),
            pltpu.VMEM((hk, HD, G * rows), jnp.bfloat16),
            pltpu.VMEM((hk, HD, G * rows), jnp.float32),
            pltpu.VMEM((hk, 1, G * rows), jnp.float32),
            pltpu.VMEM((hk, 1, G * rows), jnp.float32),
            pltpu.VMEM((rows, width), jnp.bfloat16),
            pltpu.VMEM((2 * rows, rows), jnp.float32),
            pltpu.VMEM((1, rows), jnp.int32),
            dma((3,)),
            dma((hk,)),
            dma((2, max(nh - 1, 1))),
            dma((2, max(nh - 1, 1))),
            dma((3, nseq, 2)),
            dma((nseq, 2)),
        ],
        compiler_params=pltpu.CompilerParams(
            collective_id=0, has_side_effects=True, vmem_limit_bytes=48 * 1024 * 1024
        ),
        cost_estimate=pl.CostEstimate(
            flops=4 * rows * width * 2 * rows * (reach + 1),
            bytes_accessed=4 * rows * width,
            transcendentals=0,
        ),
        name="attend",
    )(
        doc_lengths,
        queries,
        key_tokens,
        value_tokens,
        key_scales,
        value_scales,
        value_means.reshape(1, cols),
    )


def solution(mesh):
    in_specs = (
        P("seq", "head"),
        P(("seq", "head"), None),
        P(("seq", "head"), None),
        P("seq", "head"),
        P("seq", "head"),
        P("head"),
        P(),
    )
    body = functools.partial(shards, nseq=mesh.shape["seq"], nh=mesh.shape["head"])
    return jax.shard_map(body, mesh=mesh, in_specs=in_specs, out_specs=P("seq", "head"), check_vma=False)
```

```python
import functools
import math

import jax
import jax.numpy as jnp
from jax import lax
from jax.experimental import pallas as pl
from jax.experimental.pallas import tpu as pltpu
from jax.sharding import PartitionSpec as P

QH = 64
KVH = 8
HD = 128
BLK = 64
G = QH // KVH
NEG = -1e30
MESH = pl.DeviceIdType.MESH
SCALE = math.log2(math.e) / math.sqrt(HD)


def kernel(
    dims,
    doc_hbm,
    q_hbm,
    k_hbm,
    v_hbm,
    ks_hbm,
    vs_hbm,
    mean_hbm,
    out_ref,
    buf,
    q_vm,
    doc_ref,
    ks_ref,
    vs_ref,
    mean_ref,
    qt,
    acc,
    m_ref,
    mean_t,
    bias,
    lo_ref,
    local_sem,
    head_send,
    head_recv,
    send,
    recv,
):
    planes, nh, rows, hk, toks, reach = dims
    cols = hk * HD
    s = lax.axis_index("seq")
    h = lax.axis_index("head")
    z, x, c = s // 4, (s // 2) % 2, s % 2
    g = s // 2
    zdst, xdst, cdst = s + 4, s + 2 - 4 * x, s + 1 - 2 * c

    barrier = pltpu.get_barrier_semaphore()

    def greet(seq, head):
        pl.semaphore_signal(barrier, inc=1, device_id=(seq, head), device_id_type=MESH)

    for step in range(1, nh):
        greet(s, (h + step) % nh)
    greet(xdst, h)
    greet(cdst, h)

    @pl.when(z > 0)
    def _():
        greet(s - 4, h)

    @pl.when(z < planes - 1)
    def _():
        greet(s + 4, h)

    small = []
    for n, (src, dst) in enumerate(
        ((ks_hbm, ks_ref), (vs_hbm, vs_ref), (doc_hbm, doc_ref), (mean_hbm, mean_ref))
    ):
        small.append(pltpu.make_async_copy(src, dst, local_sem.at[3 + n]))
        small[-1].start()
    own_cols = pl.ds(pl.multiple_of(h * cols, HD), cols)
    locals_ = []
    for piece, hbm in enumerate((k_hbm, v_hbm)):
        dst = buf.at[s, pl.ds(pl.multiple_of(piece * rows + h * toks, 16), toks)]
        locals_.append(pltpu.make_async_copy(hbm.at[:, own_cols], dst, local_sem.at[1 + piece]))
        locals_[-1].start()

    q_copy = pltpu.make_async_copy(q_hbm, q_vm, local_sem.at[0])
    q_copy.start()
    pl.semaphore_wait(
        barrier,
        nh + 1 + jnp.where(z > 0, 1, 0) + jnp.where(z < planes - 1, 1, 0),
    )

    head_copies = []
    for piece, hbm in enumerate((k_hbm, v_hbm)):
        for step in range(1, nh):
            peer = (h + step) % nh
            peer_cols = pl.ds(pl.multiple_of(peer * cols, HD), cols)
            dst = buf.at[s, pl.ds(pl.multiple_of(piece * rows + h * toks, 16), toks)]
            head_copies.append(
                pltpu.make_async_remote_copy(
                    src_ref=hbm.at[:, peer_cols],
                    dst_ref=dst,
                    send_sem=head_send.at[piece, step - 1],
                    recv_sem=head_recv.at[piece, step - 1],
                    device_id=(s, peer),
                    device_id_type=MESH,
                )
            )
            head_copies[-1].start()

    per = rows // BLK
    pieces = []
    small[0].wait()
    small[1].wait()
    for ref in (ks_ref, vs_ref):
        sc = ref[...].astype(jnp.float32)
        pieces.append(
            jnp.concatenate(
                [jnp.broadcast_to(sc[:, i : i + 1], (per, HD)) for i in range(hk)], axis=1
            )
        )
    pieces.append(jnp.zeros((16 - 2 * per, cols), jnp.float32))
    buf[s, 2 * rows :, :] = jnp.concatenate(pieces, axis=0).astype(jnp.bfloat16)

    def part(slot, p):
        if p == 0:
            return buf.at[slot, pl.ds(0, rows)]
        return buf.at[slot, pl.ds(rows, rows + 16)]

    def copy(kind, slot, p, dst):
        return pltpu.make_async_remote_copy(
            src_ref=part(slot, p),
            dst_ref=part(slot, p),
            send_sem=send.at[kind, slot, p],
            recv_sem=recv.at[slot, p],
            device_id=(dst, h),
            device_id_type=MESH,
        )

    def need(g0, at):
        return (g0 >= 0) & (g0 <= at) & (g0 >= at - reach)

    def routes(g0, chain):
        out = [(2, need(g0, g), cdst)]
        if chain:
            up = (z + 1 < planes) & (g0 >= 0) & (g0 >= 2 * (z + 1) - reach)
            across = need(g0, 2 * z + 1 - x)
            out = [(0, up, zdst), (1, across, xdst)] + out
        return out

    def forward(g0, chain, p):
        for kind, cond, dst in routes(g0, chain):

            @pl.when(cond)
            def _(kind=kind, dst=dst):
                copy(kind, g0 * 2 + c, p, dst).start()

    def drain(g0, chain):
        for kind, cond, dst in routes(g0, chain):

            @pl.when(cond)
            def _(kind=kind, dst=dst):
                for p in range(2):
                    copy(kind, g0 * 2 + c, p, dst).wait_send()

    def arrive(slot, p):
        copy(2, slot, p, cdst).wait_recv()

    for piece in range(2):
        locals_[piece].wait()
        for step in range(1, nh):
            head_copies[piece * (nh - 1) + step - 1].wait_recv()
        forward(g, True, piece)

    small[2].wait()
    small[3].wait()
    pos = s * rows + lax.broadcasted_iota(jnp.int32, (1, rows), 1)
    start = jnp.int32(0)
    low = jnp.zeros((1, rows), jnp.int32)
    for j in range(doc_ref.shape[0]):
        low = jnp.where(pos >= start, start, low)
        start = start + doc_ref[j]
    lo_ref[...] = low
    m_ref[...] = jnp.full(m_ref.shape, NEG, jnp.float32)
    acc[...] = jnp.zeros(acc.shape, jnp.float32)
    q_copy.wait()
    for i in range(hk):
        for j in range(G):
            tile = q_vm[:, (i * G + j) * HD : (i * G + j + 1) * HD]
            qt[i, :, j * rows : (j + 1) * rows] = tile.T
        mean_t[i] = jnp.broadcast_to(mean_ref[:, i * HD : (i + 1) * HD], (rows, HD)).T

    keys = 2 * rows
    blocks = keys // BLK
    wide = 2 * rows

    def compute(g0):
        key_pos = g0 * keys + lax.broadcasted_iota(jnp.int32, (keys, rows), 0)
        query_pos = s * rows + lax.broadcasted_iota(jnp.int32, (keys, rows), 1)
        ok = (key_pos >= lo_ref[...]) & (key_pos <= query_pos)
        bias[...] = jnp.where(ok, 0.0, NEG)

        mask = jnp.concatenate([bias[...], bias[...]], axis=1)
        units = [(i, j) for i in range(hk) for j in range(G * rows // wide)]
        lane = lax.broadcasted_iota(jnp.int32, (1, HD), 1)
        sub = lax.broadcasted_iota(jnp.int32, (16, keys), 0)

        def head_of(i):
            lanes = slice(i * HD, (i + 1) * HD)
            k = buf[pl.ds(2 * g0, 2), 0:rows, lanes].reshape(keys, HD)
            v = buf[pl.ds(2 * g0, 2), rows : 2 * rows, lanes].reshape(keys, HD)
            sc = buf[pl.ds(2 * g0, 2), 2 * rows : 2 * rows + 16, lanes].astype(jnp.float32)
            ks = sc[:, 0:per].reshape(blocks, 1, HD) * SCALE
            vs = sc[:, per : 2 * per].reshape(blocks, 1, HD)
            inv = 1.0 / vs
            inv = jnp.concatenate(
                [jnp.where(lane < BLK, inv[2 * n], inv[2 * n + 1]) for n in range(2)], axis=1
            )
            high = inv.astype(jnp.bfloat16).astype(jnp.float32)
            both = jnp.where(sub == 0, high, jnp.where(sub == 1, inv - high, 0.0))
            vt = jnp.concatenate([v.T, both.astype(jnp.bfloat16)], axis=0)
            lvs = jnp.log2(vs)
            ks = jnp.concatenate([ks, ks], axis=2)
            lvs = jnp.concatenate([lvs, lvs], axis=2)
            return k, vt, ks, lvs

        def score(unit, head):
            i, j = unit
            return jnp.dot(
                head[0], qt[i, :, j * wide : (j + 1) * wide], preferred_element_type=jnp.float32
            )

        heads = {0: head_of(0)}
        ahead = score(units[0], heads[0])
        for n, (i, j) in enumerate(units):
            raw = ahead
            if n + 1 < len(units):
                after = units[n + 1][0]
                if after not in heads:
                    heads[after] = head_of(after)
                ahead = score(units[n + 1], heads[after])
            _, vt, ks, lvs = heads[i]
            at = slice(j * wide, (j + 1) * wide)
            sco = (raw.reshape(blocks, BLK, wide) * ks).reshape(keys, wide) + mask
            old = m_ref[i, :, at]
            new = jnp.maximum(old, jnp.max(sco, axis=0, keepdims=True))
            fac = jnp.exp2(old - new)
            m_ref[i, :, at] = new
            w = jnp.exp2(sco.reshape(blocks, BLK, wide) - (new.reshape(1, 1, wide) - lvs))
            wb = w.reshape(keys, wide).astype(jnp.bfloat16)
            got = jnp.dot(vt, wb, preferred_element_type=jnp.float32)
            acc[i, :, at] = acc[i, :, at] * fac + got[: HD + 8]

    def sibling(g0):
        for p in range(2):
            arrive(g0 * 2 + 1 - c, p)

    def across_block(dz):
        g0 = 2 * (z - dz) + 1 - x

        @pl.when(need(g0, g))
        def _():
            for p in range(2):
                arrive(g0 * 2 + c, p)
                forward(g0, False, p)
            sibling(g0)
            compute(g0)

    sibling(g)
    compute(g)
    last = (reach + 1) // 2

    def one_plane(dz, carry):
        g0 = 2 * (z - dz) + x

        @pl.when((g0 >= 0) & (g0 >= 2 * z - reach))
        def _():
            for p in range(2):
                arrive(g0 * 2 + c, p)
                forward(g0, True, p)

        across_block(dz - 1)

        @pl.when(need(g0, g))
        def _():
            sibling(g0)
            compute(g0)

        return carry

    lax.fori_loop(1, last + 1, one_plane, 0)
    across_block(last)

    for i in range(hk):
        for j in range(G):
            at = slice(j * rows, (j + 1) * rows)
            total = acc[i, HD : HD + 1, at] + acc[i, HD + 1 : HD + 2, at]
            o = acc[i, :HD, at] * (1.0 / total) + mean_t[i]
            out_ref[:, (i * G + j) * HD : (i * G + j + 1) * HD] = o.astype(jnp.bfloat16).T

    for one in head_copies:
        one.wait_send()

    def settle(dz, carry):
        g0 = 2 * (z - dz) + x

        @pl.when((dz == 0) | (g0 >= 0) & (g0 >= 2 * z - reach))
        def _():
            drain(g0, True)

        g1 = 2 * (z - dz) + 1 - x

        @pl.when(need(g1, g))
        def _():
            drain(g1, False)

        return carry

    lax.fori_loop(0, last + 1, settle, 0)


def shards(queries, key_tokens, value_tokens, key_scales, value_scales, value_means, doc_lengths, nseq, nh):
    rows, width = queries.shape
    toks = key_tokens.shape[0]
    hk = width // (G * HD)
    cols = hk * HD
    most = nseq * rows * 5 // 8
    window = (most - 1 + rows - 1) // rows
    reach = (window + 1) // 2
    dims = (nseq // 4, nh, rows, hk, toks, reach)
    hbm = pl.BlockSpec(memory_space=pltpu.HBM)
    vmem = pl.BlockSpec(memory_space=pltpu.VMEM)
    dma = pltpu.SemaphoreType.DMA
    return pl.pallas_call(
        functools.partial(kernel, dims),
        out_shape=jax.ShapeDtypeStruct((rows, width), jnp.bfloat16),
        in_specs=[hbm] * 7,
        out_specs=vmem,
        scratch_shapes=[
            pltpu.VMEM((nseq, 2 * rows + 16, cols), jnp.bfloat16),
            pltpu.VMEM((rows, width), jnp.bfloat16),
            pltpu.SMEM(doc_lengths.shape, jnp.int32),
            pltpu.VMEM(key_scales.shape, jnp.bfloat16),
            pltpu.VMEM(value_scales.shape, jnp.bfloat16),
            pltpu.VMEM((1, cols), jnp.float32),
            pltpu.VMEM((hk, HD, G * rows), jnp.bfloat16),
            pltpu.VMEM((hk, HD + 8, G * rows), jnp.float32),
            pltpu.VMEM((hk, 1, G * rows), jnp.float32),
            pltpu.VMEM((hk, HD, rows), jnp.float32),
            pltpu.VMEM((2 * rows, rows), jnp.float32),
            pltpu.VMEM((1, rows), jnp.int32),
            dma((7,)),
            dma((2, max(nh - 1, 1))),
            dma((2, max(nh - 1, 1))),
            dma((3, nseq, 2)),
            dma((nseq, 2)),
        ],
        compiler_params=pltpu.CompilerParams(
            collective_id=0, has_side_effects=True, vmem_limit_bytes=62 * 1024 * 1024
        ),
        cost_estimate=pl.CostEstimate(
            flops=4 * rows * width * 2 * rows * (reach + 1),
            bytes_accessed=4 * rows * width,
            transcendentals=0,
        ),
        name="attend",
    )(
        doc_lengths,
        queries,
        key_tokens,
        value_tokens,
        key_scales,
        value_scales,
        value_means.reshape(1, cols),
    )


def solution(mesh):
    in_specs = (
        P("seq", "head"),
        P(("seq", "head"), None),
        P(("seq", "head"), None),
        P("seq", "head"),
        P("seq", "head"),
        P("head"),
        P(),
    )
    body = functools.partial(shards, nseq=mesh.shape["seq"], nh=mesh.shape["head"])
    return jax.shard_map(body, mesh=mesh, in_specs=in_specs, out_specs=P("seq", "head"), check_vma=False)
```

```python
import functools
import math

import jax
import jax.numpy as jnp
from jax import lax
from jax.experimental import pallas as pl
from jax.experimental.pallas import tpu as pltpu
from jax.sharding import PartitionSpec as P

QH = 64
KVH = 8
HD = 128
BLK = 64
G = QH // KVH
NEG = -1e30
MESH = pl.DeviceIdType.MESH
SCALE = math.log2(math.e) / math.sqrt(HD)


def kernel(
    dims,
    doc_hbm,
    q_hbm,
    k_hbm,
    v_hbm,
    ks_hbm,
    vs_hbm,
    mean_hbm,
    out_ref,
    buf,
    q_vm,
    doc_ref,
    ks_ref,
    vs_ref,
    mean_ref,
    qt,
    acc,
    m_ref,
    mean_t,
    bias,
    lo_ref,
    local_sem,
    own_sem,
    head_send,
    head_recv,
    send,
    recv,
):
    planes, nh, rows, hk, toks, reach = dims
    cols = hk * HD
    s = lax.axis_index("seq")
    h = lax.axis_index("head")
    z, x, c = s // 4, (s // 2) % 2, s % 2
    g = s // 2
    zdst, xdst, cdst = s + 4, s + 2 - 4 * x, s + 1 - 2 * c

    barrier = pltpu.get_barrier_semaphore()

    def greet(seq, head):
        pl.semaphore_signal(barrier, inc=1, device_id=(seq, head), device_id_type=MESH)

    for step in range(1, nh):
        greet(s, (h + step) % nh)
    greet(xdst, h)
    greet(cdst, h)

    @pl.when(z > 0)
    def _():
        greet(s - 4, h)

    @pl.when(z < planes - 1)
    def _():
        greet(s + 4, h)

    small = []
    for n, (src, dst) in enumerate(
        ((ks_hbm, ks_ref), (vs_hbm, vs_ref), (doc_hbm, doc_ref), (mean_hbm, mean_ref))
    ):
        small.append(pltpu.make_async_copy(src, dst, local_sem.at[3 + n]))
        small[-1].start()
    def own_part(piece, i):
        return buf.at[s, i, pl.ds(pl.multiple_of(piece * rows + h * toks, 16), toks)]

    def columns(owner, i):
        return pl.ds(pl.multiple_of(owner * cols + i * HD, HD), HD)

    locals_ = {}
    for i in range(hk):
        for piece, hbm in enumerate((k_hbm, v_hbm)):
            locals_[piece, i] = pltpu.make_async_copy(
                hbm.at[:, columns(h, i)], own_part(piece, i), own_sem.at[piece, i]
            )
            locals_[piece, i].start()

    q_copy = pltpu.make_async_copy(q_hbm, q_vm, local_sem.at[0])
    q_copy.start()
    pl.semaphore_wait(
        barrier,
        nh + 1 + jnp.where(z > 0, 1, 0) + jnp.where(z < planes - 1, 1, 0),
    )

    head_copies = {}
    for i in range(hk):
        for piece, hbm in enumerate((k_hbm, v_hbm)):
            for step in range(1, nh):
                peer = (h + step) % nh
                one = pltpu.make_async_remote_copy(
                    src_ref=hbm.at[:, columns(peer, i)],
                    dst_ref=own_part(piece, i),
                    send_sem=head_send.at[piece, i, step - 1],
                    recv_sem=head_recv.at[piece, i, step - 1],
                    device_id=(s, peer),
                    device_id_type=MESH,
                )
                head_copies[piece, i, step] = one
                one.start()

    per = rows // BLK
    small[0].wait()
    small[1].wait()
    both_scales = [ref[...].astype(jnp.float32) for ref in (ks_ref, vs_ref)]
    for i in range(hk):
        scale_rows = [jnp.broadcast_to(sc[:, i : i + 1], (per, HD)) for sc in both_scales]
        scale_rows.append(jnp.zeros((16 - 2 * per, HD), jnp.float32))
        buf[s, i, 2 * rows :, :] = jnp.concatenate(scale_rows, axis=0).astype(jnp.bfloat16)

    def part(slot, p):
        return buf.at[slot, p]

    def copy(kind, slot, p, dst):
        return pltpu.make_async_remote_copy(
            src_ref=part(slot, p),
            dst_ref=part(slot, p),
            send_sem=send.at[kind, slot, p],
            recv_sem=recv.at[slot, p],
            device_id=(dst, h),
            device_id_type=MESH,
        )

    def need(g0, at):
        return (g0 >= 0) & (g0 <= at) & (g0 >= at - reach)

    def other_way(g0, plane):
        return (c == 0) & (g0 == 2 * plane - reach)

    def held(g0):
        return (g0 >= 0) & (g0 >= 2 * z - reach) & ((x == 0) | jnp.logical_not(other_way(g0, z)))

    def routes(g0, chain):
        out = [(2, need(g0, g), cdst)]
        top = z + 1 < planes
        turned = other_way(g0, z + 1)
        if chain:
            up = top & (g0 >= 0) & (g0 >= 2 * (z + 1) - reach)
            up = up & ((x == 0) | jnp.logical_not(turned))
            across = need(g0, 2 * z + 1 - x)
            return [(0, up, zdst), (1, across, xdst)] + out
        return [(0, top & (x == 0) & turned & need(g0, g), zdst)] + out

    def forward(g0, chain, p):
        for kind, cond, dst in routes(g0, chain):

            @pl.when(cond)
            def _(kind=kind, dst=dst):
                copy(kind, g0 * 2 + c, p, dst).start()

    def drain(g0, chain, pieces, kinds=(0, 1, 2)):
        for kind, cond, dst in routes(g0, chain):
            if kind not in kinds:
                continue

            @pl.when(cond)
            def _(kind=kind, dst=dst):
                for p in pieces:
                    copy(kind, g0 * 2 + c, p, dst).wait_send()

    def arrive(slot, p):
        copy(2, slot, p, cdst).wait_recv()

    def own_piece(i):
        for piece in range(2):
            locals_[piece, i].wait()
            for step in range(1, nh):
                head_copies[piece, i, step].wait_recv()
        forward(g, True, i)

    own_piece(0)

    small[2].wait()
    small[3].wait()
    pos = s * rows + lax.broadcasted_iota(jnp.int32, (1, rows), 1)
    start = jnp.int32(0)
    low = jnp.zeros((1, rows), jnp.int32)
    for j in range(doc_ref.shape[0]):
        low = jnp.where(pos >= start, start, low)
        start = start + doc_ref[j]
    lo_ref[...] = low
    m_ref[...] = jnp.full(m_ref.shape, NEG, jnp.float32)
    acc[...] = jnp.zeros(acc.shape, jnp.float32)
    q_copy.wait()
    for i in range(hk):
        for j in range(G):
            tile = q_vm[:, (i * G + j) * HD : (i * G + j + 1) * HD]
            qt[i, :, j * rows : (j + 1) * rows] = tile.T
        mean_t[i] = jnp.broadcast_to(mean_ref[:, i * HD : (i + 1) * HD], (rows, HD)).T

    keys = 2 * rows
    blocks = keys // BLK
    wide = 2 * rows

    def set_mask(g0):
        key_pos = g0 * keys + lax.broadcasted_iota(jnp.int32, (keys, rows), 0)
        query_pos = s * rows + lax.broadcasted_iota(jnp.int32, (keys, rows), 1)
        ok = (key_pos >= lo_ref[...]) & (key_pos <= query_pos)
        bias[...] = jnp.where(ok, 0.0, NEG)

    def compute(g0, i):
        mask = jnp.concatenate([bias[...], bias[...]], axis=1)
        units = [(i, j) for j in range(G * rows // wide)]
        lane = lax.broadcasted_iota(jnp.int32, (1, HD), 1)
        sub = lax.broadcasted_iota(jnp.int32, (16, keys), 0)

        def head_of(i):
            k = buf[pl.ds(2 * g0, 2), i, 0:rows, :].reshape(keys, HD)
            v = buf[pl.ds(2 * g0, 2), i, rows : 2 * rows, :].reshape(keys, HD)
            sc = buf[pl.ds(2 * g0, 2), i, 2 * rows : 2 * rows + 16, :].astype(jnp.float32)
            ks = sc[:, 0:per].reshape(blocks, 1, HD) * SCALE
            vs = sc[:, per : 2 * per].reshape(blocks, 1, HD)
            inv = 1.0 / vs
            inv = jnp.concatenate(
                [jnp.where(lane < BLK, inv[2 * n], inv[2 * n + 1]) for n in range(2)], axis=1
            )
            high = inv.astype(jnp.bfloat16).astype(jnp.float32)
            both = jnp.where(sub == 0, high, jnp.where(sub == 1, inv - high, 0.0))
            vt = jnp.concatenate([v.T, both.astype(jnp.bfloat16)], axis=0)
            lvs = jnp.log2(vs)
            ks = jnp.concatenate([ks, ks], axis=2)
            lvs = jnp.concatenate([lvs, lvs], axis=2)
            return k, vt, ks, lvs

        def score(unit, head):
            i, j = unit
            return jnp.dot(
                head[0], qt[i, :, j * wide : (j + 1) * wide], preferred_element_type=jnp.float32
            )

        head = head_of(i)
        _, vt, ks, lvs = head
        ahead = score(units[0], head)
        for n, (i, j) in enumerate(units):
            raw = ahead
            if n + 1 < len(units):
                ahead = score(units[n + 1], head)
            at = slice(j * wide, (j + 1) * wide)
            sco = (raw.reshape(blocks, BLK, wide) * ks).reshape(keys, wide) + mask
            old = m_ref[i, :, at]
            new = jnp.maximum(old, jnp.max(sco, axis=0, keepdims=True))
            fac = jnp.exp2(old - new)
            m_ref[i, :, at] = new
            w = jnp.exp2(sco.reshape(blocks, BLK, wide) - (new.reshape(1, 1, wide) - lvs))
            wb = w.reshape(keys, wide).astype(jnp.bfloat16)
            got = jnp.dot(vt, wb, preferred_element_type=jnp.float32)
            acc[i, :, at] = acc[i, :, at] * fac + got[: HD + 8]

    def sibling(g0, p):
        arrive(g0 * 2 + 1 - c, p)

    def across_piece(g0, p):
        @pl.when(need(g0, g))
        def _():
            arrive(g0 * 2 + c, p)
            forward(g0, False, p)
            sibling(g0, p)
            if p == 0:
                set_mask(g0)
            compute(g0, p)

    set_mask(g)
    for i in range(hk):
        if i + 1 < hk:
            drain(g, True, (i,), (0, 1))
            own_piece(i + 1)
        sibling(g, i)
        compute(g, i)
    last = (reach + 1) // 2

    def one_plane(dz, carry):
        g0 = 2 * (z - dz) + x
        g1 = 2 * (z - dz + 1) + 1 - x
        for p in range(hk):

            @pl.when(held(g0))
            def _(p=p):
                arrive(g0 * 2 + c, p)
                forward(g0, True, p)

            across_piece(g1, p)

        @pl.when(need(g0, g))
        def _():
            set_mask(g0)
            for p in range(hk):
                sibling(g0, p)
                compute(g0, p)

        return carry

    lax.fori_loop(1, last + 1, one_plane, 0)
    for p in range(hk):
        across_piece(2 * (z - last) + 1 - x, p)

    for i in range(hk):
        for j in range(G):
            at = slice(j * rows, (j + 1) * rows)
            total = acc[i, HD : HD + 1, at] + acc[i, HD + 1 : HD + 2, at]
            o = acc[i, :HD, at] * (1.0 / total) + mean_t[i]
            out_ref[:, (i * G + j) * HD : (i * G + j + 1) * HD] = o.astype(jnp.bfloat16).T

    for one in head_copies.values():
        one.wait_send()

    drain(g, True, (hk - 1,), (0, 1))
    drain(g, True, range(hk), (2,))

    def settle(dz, carry):
        g0 = 2 * (z - dz) + x

        @pl.when((dz > 0) & held(g0))
        def _():
            drain(g0, True, range(hk))

        g1 = 2 * (z - dz) + 1 - x

        @pl.when(need(g1, g))
        def _():
            drain(g1, False, range(hk))

        return carry

    lax.fori_loop(0, last + 1, settle, 0)


def shards(queries, key_tokens, value_tokens, key_scales, value_scales, value_means, doc_lengths, nseq, nh):
    rows, width = queries.shape
    toks = key_tokens.shape[0]
    hk = width // (G * HD)
    cols = hk * HD
    most = nseq * rows * 5 // 8
    window = (most - 1 + rows - 1) // rows
    reach = (window + 1) // 2
    dims = (nseq // 4, nh, rows, hk, toks, reach)
    hbm = pl.BlockSpec(memory_space=pltpu.HBM)
    vmem = pl.BlockSpec(memory_space=pltpu.VMEM)
    dma = pltpu.SemaphoreType.DMA
    return pl.pallas_call(
        functools.partial(kernel, dims),
        out_shape=jax.ShapeDtypeStruct((rows, width), jnp.bfloat16),
        in_specs=[hbm] * 7,
        out_specs=vmem,
        scratch_shapes=[
            pltpu.VMEM((nseq, hk, 2 * rows + 16, HD), jnp.bfloat16),
            pltpu.VMEM((rows, width), jnp.bfloat16),
            pltpu.SMEM(doc_lengths.shape, jnp.int32),
            pltpu.VMEM(key_scales.shape, jnp.bfloat16),
            pltpu.VMEM(value_scales.shape, jnp.bfloat16),
            pltpu.VMEM((1, cols), jnp.float32),
            pltpu.VMEM((hk, HD, G * rows), jnp.bfloat16),
            pltpu.VMEM((hk, HD + 8, G * rows), jnp.float32),
            pltpu.VMEM((hk, 1, G * rows), jnp.float32),
            pltpu.VMEM((hk, HD, rows), jnp.float32),
            pltpu.VMEM((2 * rows, rows), jnp.float32),
            pltpu.VMEM((1, rows), jnp.int32),
            dma((7,)),
            dma((2, hk)),
            dma((2, hk, max(nh - 1, 1))),
            dma((2, hk, max(nh - 1, 1))),
            dma((3, nseq, hk)),
            dma((nseq, hk)),
        ],
        compiler_params=pltpu.CompilerParams(
            collective_id=0, has_side_effects=True, vmem_limit_bytes=62 * 1024 * 1024
        ),
        cost_estimate=pl.CostEstimate(
            flops=4 * rows * width * 2 * rows * (reach + 1),
            bytes_accessed=4 * rows * width,
            transcendentals=0,
        ),
        name="attend",
    )(
        doc_lengths,
        queries,
        key_tokens,
        value_tokens,
        key_scales,
        value_scales,
        value_means.reshape(1, cols),
    )


def solution(mesh):
    in_specs = (
        P("seq", "head"),
        P(("seq", "head"), None),
        P(("seq", "head"), None),
        P("seq", "head"),
        P("seq", "head"),
        P("head"),
        P(),
    )
    body = functools.partial(shards, nseq=mesh.shape["seq"], nh=mesh.shape["head"])
    return jax.shard_map(body, mesh=mesh, in_specs=in_specs, out_specs=P("seq", "head"), check_vma=False)
```

```python
import functools
import math

import jax
import jax.numpy as jnp
from jax import lax
from jax.experimental import pallas as pl
from jax.experimental.pallas import tpu as pltpu
from jax.sharding import PartitionSpec as P

QH = 64
KVH = 8
HD = 128
BLK = 64
G = QH // KVH
NEG = -1e30
MESH = pl.DeviceIdType.MESH
SCALE = math.log2(math.e) / math.sqrt(HD)


def kernel(
    dims,
    doc_hbm,
    q_hbm,
    k_hbm,
    v_hbm,
    ks_hbm,
    vs_hbm,
    mean_hbm,
    out_ref,
    buf,
    q_vm,
    doc_ref,
    ks_ref,
    vs_ref,
    mean_ref,
    qs,
    acc,
    m_ref,
    s_scr,
    p_scr,
    f_scr,
    bias,
    lo_ref,
    local_sem,
    own_sem,
    head_send,
    head_recv,
    send,
    recv,
):
    planes, nh, rows, hk, toks, reach = dims
    pp = math.gcd(hk, 2)
    np_ = hk // pp
    cols = hk * HD
    s = lax.axis_index("seq")
    h = lax.axis_index("head")
    z, x, c = s // 4, (s // 2) % 2, s % 2
    g = s // 2
    zdst, xdst, cdst = s + 4, s + 2 - 4 * x, s + 1 - 2 * c

    barrier = pltpu.get_barrier_semaphore()

    def greet(seq, head):
        pl.semaphore_signal(barrier, inc=1, device_id=(seq, head), device_id_type=MESH)

    for step in range(1, nh):
        greet(s, (h + step) % nh)
    greet(xdst, h)
    greet(cdst, h)

    @pl.when(z > 0)
    def _():
        greet(s - 4, h)

    @pl.when(z < planes - 1)
    def _():
        greet(s + 4, h)

    small = []
    for n, (src, dst) in enumerate(
        ((ks_hbm, ks_ref), (vs_hbm, vs_ref), (doc_hbm, doc_ref), (mean_hbm, mean_ref))
    ):
        small.append(pltpu.make_async_copy(src, dst, local_sem.at[3 + n]))
        small[-1].start()
    def own_part(piece, i):
        return buf.at[s, i, pl.ds(pl.multiple_of(piece * rows + h * toks, 16), toks)]

    def columns(owner, i):
        return pl.ds(pl.multiple_of(owner * cols + i * HD, HD), HD)

    locals_ = {}
    for i in range(hk):
        for piece, hbm in enumerate((k_hbm, v_hbm)):
            locals_[piece, i] = pltpu.make_async_copy(
                hbm.at[:, columns(h, i)], own_part(piece, i), own_sem.at[piece, i]
            )
            locals_[piece, i].start()

    q_copy = pltpu.make_async_copy(q_hbm, q_vm, local_sem.at[0])
    q_copy.start()
    pl.semaphore_wait(
        barrier,
        nh + 1 + jnp.where(z > 0, 1, 0) + jnp.where(z < planes - 1, 1, 0),
    )

    head_copies = {}
    for i in range(hk):
        for piece, hbm in enumerate((k_hbm, v_hbm)):
            for step in range(1, nh):
                peer = (h + step) % nh
                one = pltpu.make_async_remote_copy(
                    src_ref=hbm.at[:, columns(peer, i)],
                    dst_ref=own_part(piece, i),
                    send_sem=head_send.at[piece, i, step - 1],
                    recv_sem=head_recv.at[piece, i, step - 1],
                    device_id=(s, peer),
                    device_id_type=MESH,
                )
                head_copies[piece, i, step] = one
                one.start()

    per = rows // BLK
    small[0].wait()
    small[1].wait()
    both_scales = [ref[...].astype(jnp.float32) for ref in (ks_ref, vs_ref)]
    for i in range(hk):
        scale_rows = [jnp.broadcast_to(sc[:, i : i + 1], (per, HD)) for sc in both_scales]
        scale_rows.append(jnp.zeros((16 - 2 * per, HD), jnp.float32))
        buf[s, i, 2 * rows :, :] = jnp.concatenate(scale_rows, axis=0).astype(jnp.bfloat16)

    def part(slot, p):
        return buf.at[slot, pl.ds(p * pp, pp)]

    def copy(kind, slot, p, dst):
        return pltpu.make_async_remote_copy(
            src_ref=part(slot, p),
            dst_ref=part(slot, p),
            send_sem=send.at[kind, slot, p],
            recv_sem=recv.at[slot, p],
            device_id=(dst, h),
            device_id_type=MESH,
        )

    def need(g0, at):
        return (g0 >= 0) & (g0 <= at) & (g0 >= at - reach)

    def other_way(g0, plane):
        return (c == 0) & (g0 == 2 * plane - reach)

    def held(g0):
        return (g0 >= 0) & (g0 >= 2 * z - reach) & ((x == 0) | jnp.logical_not(other_way(g0, z)))

    def routes(g0, chain):
        out = [(2, need(g0, g), cdst)]
        top = z + 1 < planes
        turned = other_way(g0, z + 1)
        if chain:
            up = top & (g0 >= 0) & (g0 >= 2 * (z + 1) - reach)
            up = up & ((x == 0) | jnp.logical_not(turned))
            across = need(g0, 2 * z + 1 - x)
            return [(0, up, zdst), (1, across, xdst)] + out
        return [(0, top & (x == 0) & turned & need(g0, g), zdst)] + out

    def forward(g0, chain, p):
        for kind, cond, dst in routes(g0, chain):

            @pl.when(cond)
            def _(kind=kind, dst=dst):
                copy(kind, g0 * 2 + c, p, dst).start()

    def drain(g0, chain, pieces, kinds=(0, 1, 2)):
        for kind, cond, dst in routes(g0, chain):
            if kind not in kinds:
                continue

            @pl.when(cond)
            def _(kind=kind, dst=dst):
                for p in pieces:
                    copy(kind, g0 * 2 + c, p, dst).wait_send()

    def arrive(slot, p):
        copy(2, slot, p, cdst).wait_recv()

    def own_piece(i):
        for j in range(i * pp, (i + 1) * pp):
            for piece in range(2):
                locals_[piece, j].wait()
                for step in range(1, nh):
                    head_copies[piece, j, step].wait_recv()
        forward(g, True, i)

    own_piece(0)

    small[2].wait()
    small[3].wait()
    pos = s * rows + lax.broadcasted_iota(jnp.int32, (rows, 1), 0)
    start = jnp.int32(0)
    low = jnp.zeros((rows, 1), jnp.int32)
    for j in range(doc_ref.shape[0]):
        low = jnp.where(pos >= start, start, low)
        start = start + doc_ref[j]
    lo_ref[...] = jnp.broadcast_to(low, lo_ref.shape)
    m_ref[...] = jnp.full(m_ref.shape, NEG, jnp.float32)
    acc[...] = jnp.zeros(acc.shape, jnp.float32)
    q_copy.wait()
    for i in range(hk):
        for j in range(G):
            qs[i, j * rows : (j + 1) * rows, :] = q_vm[:, (i * G + j) * HD : (i * G + j + 1) * HD]

    keys = 2 * rows
    blocks = keys // BLK
    lane = lax.broadcasted_iota(jnp.int32, (1, HD), 1)

    def set_mask(g0):
        key_pos = g0 * keys + lax.broadcasted_iota(jnp.int32, (rows, keys), 1)
        query_pos = s * rows + lax.broadcasted_iota(jnp.int32, (rows, keys), 0)
        low = jnp.concatenate([lo_ref[...], lo_ref[...]], axis=1)
        ok = (key_pos >= low) & (key_pos <= query_pos)
        bias[...] = jnp.where(ok, 0.0, NEG)

    def compute(g0, p):
        heads = range(p * pp, (p + 1) * pp)

        def along(sc):
            return jnp.concatenate(
                [jnp.where(lane < BLK, sc[n // per, n % per][None], sc[n // per, n % per + 1][None])
                 for n in range(0, blocks, 2)],
                axis=1,
            )

        rows_of, values = {}, {}
        for i in heads:
            k = buf[pl.ds(2 * g0, 2), i, 0:rows, :].reshape(keys, HD)
            s_scr[i % pp] = lax.dot_general(
                qs[i], k, (((1,), (1,)), ((), ())), preferred_element_type=jnp.float32
            )
            v = buf[pl.ds(2 * g0, 2), i, rows : 2 * rows, :].reshape(keys, HD)
            sc = buf[pl.ds(2 * g0, 2), i, 2 * rows : 2 * rows + 16, :].astype(jnp.float32)
            vs = sc[:, per : 2 * per]
            rows_of[i] = (along(sc[:, 0:per] * SCALE), along(jnp.log2(vs)))
            inv = 1.0 / vs.reshape(blocks, 1, HD)
            high = inv.astype(jnp.bfloat16).astype(jnp.float32)
            low = inv - high
            both = jnp.where(lane[None] == 0, high, jnp.where(lane[None] == 1, low, 0.0))
            both = jnp.broadcast_to(both, (blocks, BLK, HD)).reshape(keys, HD)
            values[i] = jnp.concatenate([v, both.astype(jnp.bfloat16)], axis=1)
        for i in heads:
            ks, lvs = rows_of[i]
            add = bias[...] + lvs
            for j in range(G):
                at = slice(j * rows, (j + 1) * rows)
                sco = s_scr[i % pp, at, :] * ks + add
                old = m_ref[i, at, :]
                new = jnp.maximum(old, jnp.max(sco, axis=1, keepdims=True))
                m_ref[i, at, :] = new
                f_scr[i % pp, at, :] = jnp.exp2(old - new)
                w = jnp.exp2(sco - jnp.concatenate([new, new], axis=1))
                p_scr[i % pp, at, :] = w.astype(jnp.bfloat16)
            got = jnp.dot(p_scr[i % pp], values[i], preferred_element_type=jnp.float32)
            fac = f_scr[i % pp]
            acc[i] = acc[i] * jnp.concatenate([fac, fac], axis=1) + got

    def sibling(g0, p):
        arrive(g0 * 2 + 1 - c, p)

    def across_piece(g0, p):
        @pl.when(need(g0, g))
        def _():
            arrive(g0 * 2 + c, p)
            forward(g0, False, p)
            sibling(g0, p)
            if p == 0:
                set_mask(g0)
            compute(g0, p)

    set_mask(g)
    for i in range(np_):
        if i + 1 < np_:
            drain(g, True, (i,), (0, 1))
            own_piece(i + 1)
        sibling(g, i)
        compute(g, i)
    last = (reach + 1) // 2

    def one_plane(dz, carry):
        g0 = 2 * (z - dz) + x
        g1 = 2 * (z - dz + 1) + 1 - x
        for p in range(np_):

            @pl.when(held(g0))
            def _(p=p):
                arrive(g0 * 2 + c, p)
                forward(g0, True, p)

            across_piece(g1, p)

        @pl.when(need(g0, g))
        def _():
            set_mask(g0)
            for p in range(np_):
                sibling(g0, p)
                compute(g0, p)

        return carry

    lax.fori_loop(1, last + 1, one_plane, 0)
    for p in range(np_):
        across_piece(2 * (z - last) + 1 - x, p)

    for i in range(hk):
        for j in range(G):
            at = slice(j * rows, (j + 1) * rows)
            total = acc[i, at, HD : HD + 1] + acc[i, at, HD + 1 : HD + 2]
            o = acc[i, at, :HD] * (1.0 / total) + mean_ref[:, i * HD : (i + 1) * HD]
            out_ref[:, (i * G + j) * HD : (i * G + j + 1) * HD] = o.astype(jnp.bfloat16)

    for one in head_copies.values():
        one.wait_send()

    drain(g, True, (np_ - 1,), (0, 1))
    drain(g, True, range(np_), (2,))

    def settle(dz, carry):
        g0 = 2 * (z - dz) + x

        @pl.when((dz > 0) & held(g0))
        def _():
            drain(g0, True, range(np_))

        g1 = 2 * (z - dz) + 1 - x

        @pl.when(need(g1, g))
        def _():
            drain(g1, False, range(np_))

        return carry

    lax.fori_loop(0, last + 1, settle, 0)


def shards(queries, key_tokens, value_tokens, key_scales, value_scales, value_means, doc_lengths, nseq, nh):
    rows, width = queries.shape
    toks = key_tokens.shape[0]
    hk = width // (G * HD)
    cols = hk * HD
    most = nseq * rows * 5 // 8
    window = (most - 1 + rows - 1) // rows
    reach = (window + 1) // 2
    dims = (nseq // 4, nh, rows, hk, toks, reach)
    hbm = pl.BlockSpec(memory_space=pltpu.HBM)
    vmem = pl.BlockSpec(memory_space=pltpu.VMEM)
    dma = pltpu.SemaphoreType.DMA
    return pl.pallas_call(
        functools.partial(kernel, dims),
        out_shape=jax.ShapeDtypeStruct((rows, width), jnp.bfloat16),
        in_specs=[hbm] * 7,
        out_specs=vmem,
        scratch_shapes=[
            pltpu.VMEM((nseq, hk, 2 * rows + 16, HD), jnp.bfloat16),
            pltpu.VMEM((rows, width), jnp.bfloat16),
            pltpu.SMEM(doc_lengths.shape, jnp.int32),
            pltpu.VMEM(key_scales.shape, jnp.bfloat16),
            pltpu.VMEM(value_scales.shape, jnp.bfloat16),
            pltpu.VMEM((1, cols), jnp.float32),
            pltpu.VMEM((hk, G * rows, HD), jnp.bfloat16),
            pltpu.VMEM((hk, G * rows, 2 * HD), jnp.float32),
            pltpu.VMEM((hk, G * rows, HD), jnp.float32),
            pltpu.VMEM((math.gcd(hk, 2), G * rows, 2 * rows), jnp.float32),
            pltpu.VMEM((math.gcd(hk, 2), G * rows, 2 * rows), jnp.bfloat16),
            pltpu.VMEM((math.gcd(hk, 2), G * rows, HD), jnp.float32),
            pltpu.VMEM((rows, 2 * rows), jnp.float32),
            pltpu.VMEM((rows, HD), jnp.int32),
            dma((7,)),
            dma((2, hk)),
            dma((2, hk, max(nh - 1, 1))),
            dma((2, hk, max(nh - 1, 1))),
            dma((3, nseq, hk)),
            dma((nseq, hk)),
        ],
        compiler_params=pltpu.CompilerParams(
            collective_id=0, has_side_effects=True, vmem_limit_bytes=62 * 1024 * 1024
        ),
        cost_estimate=pl.CostEstimate(
            flops=4 * rows * width * 2 * rows * (reach + 1),
            bytes_accessed=4 * rows * width,
            transcendentals=0,
        ),
        name="attend",
    )(
        doc_lengths,
        queries,
        key_tokens,
        value_tokens,
        key_scales,
        value_scales,
        value_means.reshape(1, cols),
    )


def solution(mesh):
    in_specs = (
        P("seq", "head"),
        P(("seq", "head"), None),
        P(("seq", "head"), None),
        P("seq", "head"),
        P("seq", "head"),
        P("head"),
        P(),
    )
    body = functools.partial(shards, nseq=mesh.shape["seq"], nh=mesh.shape["head"])
    return jax.shard_map(body, mesh=mesh, in_specs=in_specs, out_specs=P("seq", "head"), check_vma=False)
```

```python
import functools
import math

import jax
import jax.numpy as jnp
from jax import lax
from jax.experimental import pallas as pl
from jax.experimental.pallas import tpu as pltpu
from jax.sharding import PartitionSpec as P

QH = 64
KVH = 8
HD = 128
BLK = 64
G = QH // KVH
NEG = -1e30
MESH = pl.DeviceIdType.MESH
SCALE = math.log2(math.e) / math.sqrt(HD)


def kernel(
    dims,
    doc_hbm,
    q_hbm,
    k_hbm,
    v_hbm,
    ks_hbm,
    vs_hbm,
    mean_hbm,
    out_ref,
    buf,
    q_vm,
    doc_ref,
    ks_ref,
    vs_ref,
    mean_ref,
    qs,
    acc,
    m_ref,
    l_ref,
    s_scr,
    p_scr,
    f_scr,
    bias,
    lo_ref,
    local_sem,
    own_sem,
    head_send,
    head_recv,
    send,
    recv,
):
    planes, nh, rows, hk, toks, reach = dims
    pp = math.gcd(hk, 2)
    np_ = hk // pp
    cols = hk * HD
    s = lax.axis_index("seq")
    h = lax.axis_index("head")
    z, x, c = s // 4, (s // 2) % 2, s % 2
    g = s // 2
    zdst, xdst, cdst = s + 4, s + 2 - 4 * x, s + 1 - 2 * c

    barrier = pltpu.get_barrier_semaphore()

    def greet(seq, head):
        pl.semaphore_signal(barrier, inc=1, device_id=(seq, head), device_id_type=MESH)

    for step in range(1, nh):
        greet(s, (h + step) % nh)
    greet(xdst, h)
    greet(cdst, h)

    @pl.when(z > 0)
    def _():
        greet(s - 4, h)

    @pl.when(z < planes - 1)
    def _():
        greet(s + 4, h)

    small = []
    for n, (src, dst) in enumerate(
        ((ks_hbm, ks_ref), (vs_hbm, vs_ref), (doc_hbm, doc_ref), (mean_hbm, mean_ref))
    ):
        small.append(pltpu.make_async_copy(src, dst, local_sem.at[3 + n]))
        small[-1].start()
    def own_part(piece, i):
        return buf.at[s, i, pl.ds(pl.multiple_of(piece * rows + h * toks, 16), toks)]

    def columns(owner, i):
        return pl.ds(pl.multiple_of(owner * cols + i * HD, HD), HD)

    locals_ = {}
    for i in range(hk):
        for piece, hbm in enumerate((k_hbm, v_hbm)):
            locals_[piece, i] = pltpu.make_async_copy(
                hbm.at[:, columns(h, i)], own_part(piece, i), own_sem.at[piece, i]
            )
            locals_[piece, i].start()

    q_copy = pltpu.make_async_copy(q_hbm, q_vm, local_sem.at[0])
    q_copy.start()
    pl.semaphore_wait(
        barrier,
        nh + 1 + jnp.where(z > 0, 1, 0) + jnp.where(z < planes - 1, 1, 0),
    )

    head_copies = {}
    for i in range(hk):
        for piece, hbm in enumerate((k_hbm, v_hbm)):
            for step in range(1, nh):
                peer = (h + step) % nh
                one = pltpu.make_async_remote_copy(
                    src_ref=hbm.at[:, columns(peer, i)],
                    dst_ref=own_part(piece, i),
                    send_sem=head_send.at[piece, i, step - 1],
                    recv_sem=head_recv.at[piece, i, step - 1],
                    device_id=(s, peer),
                    device_id_type=MESH,
                )
                head_copies[piece, i, step] = one
                one.start()

    per = rows // BLK
    small[0].wait()
    small[1].wait()
    both_scales = [ref[...].astype(jnp.float32) for ref in (ks_ref, vs_ref)]
    for i in range(hk):
        scale_rows = [jnp.broadcast_to(sc[:, i : i + 1], (per, HD)) for sc in both_scales]
        scale_rows.append(jnp.zeros((16 - 2 * per, HD), jnp.float32))
        buf[s, i, 2 * rows :, :] = jnp.concatenate(scale_rows, axis=0).astype(jnp.bfloat16)

    def part(slot, p):
        return buf.at[slot, pl.ds(p * pp, pp)]

    def copy(kind, slot, p, dst):
        return pltpu.make_async_remote_copy(
            src_ref=part(slot, p),
            dst_ref=part(slot, p),
            send_sem=send.at[kind, slot, p],
            recv_sem=recv.at[slot, p],
            device_id=(dst, h),
            device_id_type=MESH,
        )

    def need(g0, at):
        return (g0 >= 0) & (g0 <= at) & (g0 >= at - reach)

    def other_way(g0, plane):
        return (c == 0) & (g0 == 2 * plane - reach)

    def held(g0):
        return (g0 >= 0) & (g0 >= 2 * z - reach) & ((x == 0) | jnp.logical_not(other_way(g0, z)))

    def routes(g0, chain):
        out = [(2, need(g0, g), cdst)]
        top = z + 1 < planes
        turned = other_way(g0, z + 1)
        if chain:
            up = top & (g0 >= 0) & (g0 >= 2 * (z + 1) - reach)
            up = up & ((x == 0) | jnp.logical_not(turned))
            across = need(g0, 2 * z + 1 - x)
            return [(0, up, zdst), (1, across, xdst)] + out
        return [(0, top & (x == 0) & turned & need(g0, g), zdst)] + out

    def forward(g0, chain, p):
        for kind, cond, dst in routes(g0, chain):

            @pl.when(cond)
            def _(kind=kind, dst=dst):
                copy(kind, g0 * 2 + c, p, dst).start()

    def drain(g0, chain, pieces, kinds=(0, 1, 2)):
        for kind, cond, dst in routes(g0, chain):
            if kind not in kinds:
                continue

            @pl.when(cond)
            def _(kind=kind, dst=dst):
                for p in pieces:
                    copy(kind, g0 * 2 + c, p, dst).wait_send()

    def arrive(slot, p):
        copy(2, slot, p, cdst).wait_recv()

    small[2].wait()
    small[3].wait()
    pos = s * rows + lax.broadcasted_iota(jnp.int32, (rows, 1), 0)
    start = jnp.int32(0)
    low = jnp.zeros((rows, 1), jnp.int32)
    for j in range(doc_ref.shape[0]):
        low = jnp.where(pos >= start, start, low)
        start = start + doc_ref[j]
    lo_ref[...] = jnp.broadcast_to(low, lo_ref.shape)
    m_ref[...] = jnp.full(m_ref.shape, NEG, jnp.float32)
    l_ref[...] = jnp.zeros(l_ref.shape, jnp.float32)
    acc[...] = jnp.zeros(acc.shape, jnp.float32)
    q_copy.wait()
    for i in range(hk):
        for j in range(G):
            qs[i, j * rows : (j + 1) * rows, :] = q_vm[:, (i * G + j) * HD : (i * G + j + 1) * HD]

    def own_piece(i):
        for j in range(i * pp, (i + 1) * pp):
            for piece in range(2):
                locals_[piece, j].wait()
                for step in range(1, nh):
                    head_copies[piece, j, step].wait_recv()
        forward(g, True, i)

    keys = 2 * rows
    blocks = keys // BLK
    lane = lax.broadcasted_iota(jnp.int32, (1, HD), 1)

    def set_mask(g0):
        key_pos = g0 * keys + lax.broadcasted_iota(jnp.int32, (rows, keys), 1)
        query_pos = s * rows + lax.broadcasted_iota(jnp.int32, (rows, keys), 0)
        low = jnp.concatenate([lo_ref[...], lo_ref[...]], axis=1)
        ok = (key_pos >= low) & (key_pos <= query_pos)
        bias[...] = jnp.where(ok, 0.0, NEG)

    def compute(g0, p):
        heads = range(p * pp, (p + 1) * pp)

        def along(sc):
            return jnp.concatenate(
                [jnp.where(lane < BLK, sc[n // per, n % per][None], sc[n // per, n % per + 1][None])
                 for n in range(0, blocks, 2)],
                axis=1,
            )

        rows_of, values = {}, {}
        for i in heads:
            k = buf[pl.ds(2 * g0, 2), i, 0:rows, :].reshape(keys, HD)
            s_scr[i % pp] = lax.dot_general(
                qs[i], k, (((1,), (1,)), ((), ())), preferred_element_type=jnp.float32
            )
            v = buf[pl.ds(2 * g0, 2), i, rows : 2 * rows, :].reshape(keys, HD)
            sc = buf[pl.ds(2 * g0, 2), i, 2 * rows : 2 * rows + 16, :].astype(jnp.float32)
            rows_of[i] = (along(sc[:, 0:per] * SCALE), along(sc[:, per : 2 * per]))
            values[i] = v
        for i in heads:
            ks, vs = rows_of[i]
            for j in range(G):
                at = slice(j * rows, (j + 1) * rows)
                sco = s_scr[i % pp, at, :] * ks + bias[...]
                old = m_ref[i, at, :]
                new = jnp.maximum(old, jnp.max(sco, axis=1, keepdims=True))
                m_ref[i, at, :] = new
                fac = jnp.exp2(old - new)
                f_scr[i % pp, at, :] = fac
                w = jnp.exp2(sco - jnp.concatenate([new, new], axis=1))
                l_ref[i, at, :] = l_ref[i, at, :] * fac + (w[:, :HD] + w[:, HD:])
                p_scr[i % pp, at, :] = (w * vs).astype(jnp.bfloat16)
            got = jnp.dot(p_scr[i % pp], values[i], preferred_element_type=jnp.float32)
            acc[i] = acc[i] * f_scr[i % pp] + got

    def sibling(g0, p):
        arrive(g0 * 2 + 1 - c, p)

    def across_piece(g0, p):
        @pl.when(need(g0, g))
        def _():
            arrive(g0 * 2 + c, p)
            forward(g0, False, p)
            sibling(g0, p)
            if p == 0:
                set_mask(g0)
            compute(g0, p)

    set_mask(g)
    for i in range(np_):
        if i > 0:
            drain(g, True, (i - 1,), (0, 1))
        own_piece(i)
        sibling(g, i)
        compute(g, i)
    last = (reach + 1) // 2

    def one_plane(dz, carry):
        g0 = 2 * (z - dz) + x
        g1 = 2 * (z - dz + 1) + 1 - x
        for p in range(np_):

            @pl.when(held(g0))
            def _(p=p):
                arrive(g0 * 2 + c, p)
                forward(g0, True, p)

            across_piece(g1, p)

        @pl.when(need(g0, g))
        def _():
            set_mask(g0)
            for p in range(np_):
                sibling(g0, p)
                compute(g0, p)

        return carry

    lax.fori_loop(1, last + 1, one_plane, 0)
    for p in range(np_):
        across_piece(2 * (z - last) + 1 - x, p)

    for i in range(hk):
        for j in range(G):
            at = slice(j * rows, (j + 1) * rows)
            total = jnp.sum(l_ref[i, at, :], axis=1, keepdims=True)
            o = acc[i, at, :] * (1.0 / total) + mean_ref[:, i * HD : (i + 1) * HD]
            out_ref[:, (i * G + j) * HD : (i * G + j + 1) * HD] = o.astype(jnp.bfloat16)

    for one in head_copies.values():
        one.wait_send()

    drain(g, True, (np_ - 1,), (0, 1))
    drain(g, True, range(np_), (2,))

    def settle(dz, carry):
        g0 = 2 * (z - dz) + x

        @pl.when((dz > 0) & held(g0))
        def _():
            drain(g0, True, range(np_))

        g1 = 2 * (z - dz) + 1 - x

        @pl.when(need(g1, g))
        def _():
            drain(g1, False, range(np_))

        return carry

    lax.fori_loop(0, last + 1, settle, 0)


def shards(queries, key_tokens, value_tokens, key_scales, value_scales, value_means, doc_lengths, nseq, nh):
    rows, width = queries.shape
    toks = key_tokens.shape[0]
    hk = width // (G * HD)
    cols = hk * HD
    most = nseq * rows * 5 // 8
    window = (most - 1 + rows - 1) // rows
    reach = (window + 1) // 2
    dims = (nseq // 4, nh, rows, hk, toks, reach)
    hbm = pl.BlockSpec(memory_space=pltpu.HBM)
    vmem = pl.BlockSpec(memory_space=pltpu.VMEM)
    dma = pltpu.SemaphoreType.DMA
    return pl.pallas_call(
        functools.partial(kernel, dims),
        out_shape=jax.ShapeDtypeStruct((rows, width), jnp.bfloat16),
        in_specs=[hbm] * 7,
        out_specs=vmem,
        scratch_shapes=[
            pltpu.VMEM((nseq, hk, 2 * rows + 16, HD), jnp.bfloat16),
            pltpu.VMEM((rows, width), jnp.bfloat16),
            pltpu.SMEM(doc_lengths.shape, jnp.int32),
            pltpu.VMEM(key_scales.shape, jnp.bfloat16),
            pltpu.VMEM(value_scales.shape, jnp.bfloat16),
            pltpu.VMEM((1, cols), jnp.float32),
            pltpu.VMEM((hk, G * rows, HD), jnp.bfloat16),
            pltpu.VMEM((hk, G * rows, HD), jnp.float32),
            pltpu.VMEM((hk, G * rows, HD), jnp.float32),
            pltpu.VMEM((hk, G * rows, HD), jnp.float32),
            pltpu.VMEM((math.gcd(hk, 2), G * rows, 2 * rows), jnp.float32),
            pltpu.VMEM((math.gcd(hk, 2), G * rows, 2 * rows), jnp.bfloat16),
            pltpu.VMEM((math.gcd(hk, 2), G * rows, HD), jnp.float32),
            pltpu.VMEM((rows, 2 * rows), jnp.float32),
            pltpu.VMEM((rows, HD), jnp.int32),
            dma((7,)),
            dma((2, hk)),
            dma((2, hk, max(nh - 1, 1))),
            dma((2, hk, max(nh - 1, 1))),
            dma((3, nseq, hk)),
            dma((nseq, hk)),
        ],
        compiler_params=pltpu.CompilerParams(
            collective_id=0, has_side_effects=True, vmem_limit_bytes=62 * 1024 * 1024
        ),
        cost_estimate=pl.CostEstimate(
            flops=4 * rows * width * 2 * rows * (reach + 1),
            bytes_accessed=4 * rows * width,
            transcendentals=0,
        ),
        name="attend",
    )(
        doc_lengths,
        queries,
        key_tokens,
        value_tokens,
        key_scales,
        value_scales,
        value_means.reshape(1, cols),
    )


def solution(mesh):
    in_specs = (
        P("seq", "head"),
        P(("seq", "head"), None),
        P(("seq", "head"), None),
        P("seq", "head"),
        P("seq", "head"),
        P("head"),
        P(),
    )
    body = functools.partial(shards, nseq=mesh.shape["seq"], nh=mesh.shape["head"])
    return jax.shard_map(body, mesh=mesh, in_specs=in_specs, out_specs=P("seq", "head"), check_vma=False)
```

```python
import functools
import math

import jax
import jax.numpy as jnp
from jax import lax
from jax.experimental import pallas as pl
from jax.experimental.pallas import tpu as pltpu
from jax.sharding import PartitionSpec as P

QH = 64
KVH = 8
HD = 128
BLK = 64
G = QH // KVH
NEG = -1e30
MESH = pl.DeviceIdType.MESH
SCALE = math.log2(math.e) / math.sqrt(HD)


def kernel(
    dims,
    doc_hbm,
    q_hbm,
    k_hbm,
    v_hbm,
    ks_hbm,
    vs_hbm,
    mean_hbm,
    out_hbm,
    buf,
    q_vm,
    doc_ref,
    ks_ref,
    vs_ref,
    mean_ref,
    qs,
    acc,
    m_ref,
    l_ref,
    s_scr,
    p_scr,
    f_scr,
    out_vm,
    bias,
    lo_ref,
    local_sem,
    out_sem,
    own_sem,
    head_send,
    head_recv,
    send,
    recv,
):
    planes, nh, rows, hk, toks, reach = dims
    pp = math.gcd(hk, 2)
    np_ = hk // pp
    cols = hk * HD
    s = lax.axis_index("seq")
    h = lax.axis_index("head")
    z, x, c = s // 4, (s // 2) % 2, s % 2
    g = s // 2
    zdst, xdst, cdst = s + 4, s + 2 - 4 * x, s + 1 - 2 * c

    barrier = pltpu.get_barrier_semaphore()

    def greet(seq, head):
        pl.semaphore_signal(barrier, inc=1, device_id=(seq, head), device_id_type=MESH)

    for step in range(1, nh):
        greet(s, (h + step) % nh)
    greet(xdst, h)
    greet(cdst, h)

    @pl.when(z > 0)
    def _():
        greet(s - 4, h)

    @pl.when(z < planes - 1)
    def _():
        greet(s + 4, h)

    small = []
    for n, (src, dst) in enumerate(
        ((ks_hbm, ks_ref), (vs_hbm, vs_ref), (doc_hbm, doc_ref), (mean_hbm, mean_ref))
    ):
        small.append(pltpu.make_async_copy(src, dst, local_sem.at[3 + n]))
        small[-1].start()
    def own_part(piece, i):
        return buf.at[s, i, pl.ds(pl.multiple_of(piece * rows + h * toks, 16), toks)]

    def columns(owner, i):
        return pl.ds(pl.multiple_of(owner * cols + i * HD, HD), HD)

    locals_ = {}
    for i in range(hk):
        for piece, hbm in enumerate((k_hbm, v_hbm)):
            locals_[piece, i] = pltpu.make_async_copy(
                hbm.at[:, columns(h, i)], own_part(piece, i), own_sem.at[piece, i]
            )
            locals_[piece, i].start()

    q_copy = pltpu.make_async_copy(q_hbm, q_vm, local_sem.at[0])
    q_copy.start()
    pl.semaphore_wait(
        barrier,
        nh + 1 + jnp.where(z > 0, 1, 0) + jnp.where(z < planes - 1, 1, 0),
    )

    head_copies = {}

    def exchange(heads):
        for i in heads:
            for piece, hbm in enumerate((k_hbm, v_hbm)):
                for step in range(1, nh):
                    peer = (h + step) % nh
                    one = pltpu.make_async_remote_copy(
                        src_ref=hbm.at[:, columns(peer, i)],
                        dst_ref=own_part(piece, i),
                        send_sem=head_send.at[piece, i, step - 1],
                        recv_sem=head_recv.at[piece, i, step - 1],
                        device_id=(s, peer),
                        device_id_type=MESH,
                    )
                    head_copies[piece, i, step] = one
                    one.start()

    exchange(range(pp))

    per = rows // BLK
    small[0].wait()
    small[1].wait()
    both_scales = [ref[...].astype(jnp.float32) for ref in (ks_ref, vs_ref)]
    for i in range(hk):
        scale_rows = [jnp.broadcast_to(sc[:, i : i + 1], (per, HD)) for sc in both_scales]
        scale_rows.append(jnp.zeros((16 - 2 * per, HD), jnp.float32))
        buf[s, i, 2 * rows :, :] = jnp.concatenate(scale_rows, axis=0).astype(jnp.bfloat16)

    def part(slot, p):
        return buf.at[slot, pl.ds(p * pp, pp)]

    def copy(kind, slot, p, dst):
        return pltpu.make_async_remote_copy(
            src_ref=part(slot, p),
            dst_ref=part(slot, p),
            send_sem=send.at[kind, slot, p],
            recv_sem=recv.at[slot, p],
            device_id=(dst, h),
            device_id_type=MESH,
        )

    def need(g0, at):
        return (g0 >= 0) & (g0 <= at) & (g0 >= at - reach)

    def other_way(g0, plane):
        return (c == 0) & (g0 == 2 * plane - reach)

    def held(g0):
        return (g0 >= 0) & (g0 >= 2 * z - reach) & ((x == 0) | jnp.logical_not(other_way(g0, z)))

    def routes(g0, chain):
        out = [(2, need(g0, g), cdst)]
        top = z + 1 < planes
        turned = other_way(g0, z + 1)
        if chain:
            up = top & (g0 >= 0) & (g0 >= 2 * (z + 1) - reach)
            up = up & ((x == 0) | jnp.logical_not(turned))
            across = need(g0, 2 * z + 1 - x)
            return [(0, up, zdst), (1, across, xdst)] + out
        return [(0, top & (x == 0) & turned & need(g0, g), zdst)] + out

    def forward(g0, chain, p):
        for kind, cond, dst in routes(g0, chain):

            @pl.when(cond)
            def _(kind=kind, dst=dst):
                copy(kind, g0 * 2 + c, p, dst).start()

    def drain(g0, chain, pieces, kinds=(0, 1, 2)):
        for kind, cond, dst in routes(g0, chain):
            if kind not in kinds:
                continue

            @pl.when(cond)
            def _(kind=kind, dst=dst):
                for p in pieces:
                    copy(kind, g0 * 2 + c, p, dst).wait_send()

    def arrive(slot, p):
        copy(2, slot, p, cdst).wait_recv()

    small[2].wait()
    small[3].wait()
    pos = s * rows + lax.broadcasted_iota(jnp.int32, (rows, 1), 0)
    start = jnp.int32(0)
    low = jnp.zeros((rows, 1), jnp.int32)
    for j in range(doc_ref.shape[0]):
        low = jnp.where(pos >= start, start, low)
        start = start + doc_ref[j]
    lo_ref[...] = jnp.broadcast_to(low, lo_ref.shape)
    m_ref[...] = jnp.full(m_ref.shape, NEG, jnp.float32)
    l_ref[...] = jnp.zeros(l_ref.shape, jnp.float32)
    acc[...] = jnp.zeros(acc.shape, jnp.float32)
    q_copy.wait()
    for i in range(hk):
        for j in range(G):
            qs[i, j * rows : (j + 1) * rows, :] = q_vm[:, (i * G + j) * HD : (i * G + j + 1) * HD]

    exchange(range(pp, hk))

    def own_piece(i):
        for j in range(i * pp, (i + 1) * pp):
            for piece in range(2):
                locals_[piece, j].wait()
                for step in range(1, nh):
                    head_copies[piece, j, step].wait_recv()
        forward(g, True, i)

    keys = 2 * rows
    blocks = keys // BLK
    lane = lax.broadcasted_iota(jnp.int32, (1, HD), 1)

    def set_mask(g0):
        key_pos = g0 * keys + lax.broadcasted_iota(jnp.int32, (rows, keys), 1)
        query_pos = s * rows + lax.broadcasted_iota(jnp.int32, (rows, keys), 0)
        low = jnp.concatenate([lo_ref[...], lo_ref[...]], axis=1)
        ok = (key_pos >= low) & (key_pos <= query_pos)
        bias[...] = jnp.where(ok, 0.0, NEG)

    def compute(g0, p):
        heads = range(p * pp, (p + 1) * pp)

        def along(sc):
            return jnp.concatenate(
                [jnp.where(lane < BLK, sc[n // per, n % per][None], sc[n // per, n % per + 1][None])
                 for n in range(0, blocks, 2)],
                axis=1,
            )

        rows_of, values = {}, {}
        for i in heads:
            k = buf[pl.ds(2 * g0, 2), i, 0:rows, :].reshape(keys, HD)
            s_scr[i % pp] = lax.dot_general(
                qs[i], k, (((1,), (1,)), ((), ())), preferred_element_type=jnp.float32
            )
            v = buf[pl.ds(2 * g0, 2), i, rows : 2 * rows, :].reshape(keys, HD)
            sc = buf[pl.ds(2 * g0, 2), i, 2 * rows : 2 * rows + 16, :].astype(jnp.float32)
            rows_of[i] = (along(sc[:, 0:per] * SCALE), along(sc[:, per : 2 * per]))
            values[i] = v
        for i in heads:
            ks, vs = rows_of[i]
            for j in range(G):
                at = slice(j * rows, (j + 1) * rows)
                sco = s_scr[i % pp, at, :] * ks + bias[...]
                old = m_ref[i, at, :]
                new = jnp.maximum(old, jnp.max(sco, axis=1, keepdims=True))
                m_ref[i, at, :] = new
                fac = jnp.exp2(old - new)
                f_scr[i % pp, at, :] = fac
                w = jnp.exp2(sco - jnp.concatenate([new, new], axis=1))
                l_ref[i, at, :] = l_ref[i, at, :] * fac + (w[:, :HD] + w[:, HD:])
                p_scr[i % pp, at, :] = (w * vs).astype(jnp.bfloat16)
            got = jnp.dot(p_scr[i % pp], values[i], preferred_element_type=jnp.float32)
            acc[i] = acc[i] * f_scr[i % pp] + got

    def sibling(g0, p):
        arrive(g0 * 2 + 1 - c, p)

    def across_piece(g0, p):
        @pl.when(need(g0, g))
        def _():
            arrive(g0 * 2 + c, p)
            forward(g0, False, p)
            sibling(g0, p)
            if p == 0:
                set_mask(g0)
            compute(g0, p)

    set_mask(g)
    for i in range(np_):
        if i > 0:
            drain(g, True, (i - 1,), (0, 1))
        own_piece(i)
        sibling(g, i)
        compute(g, i)
    last = (reach + 1) // 2

    def one_plane(dz, carry):
        g0 = 2 * (z - dz) + x
        g1 = 2 * (z - dz + 1) + 1 - x
        for p in range(np_):

            @pl.when(held(g0))
            def _(p=p):
                arrive(g0 * 2 + c, p)
                forward(g0, True, p)

            across_piece(g1, p)

        @pl.when(need(g0, g))
        def _():
            set_mask(g0)
            for p in range(np_):
                sibling(g0, p)
                compute(g0, p)

        return carry

    lax.fori_loop(1, last + 1, one_plane, 0)
    outs = []
    for p in range(np_):
        across_piece(2 * (z - last) + 1 - x, p)
        for i in range(p * pp, (p + 1) * pp):
            for j in range(G):
                at = slice(j * rows, (j + 1) * rows)
                total = jnp.sum(l_ref[i, at, :], axis=1, keepdims=True)
                o = acc[i, at, :] * (1.0 / total) + mean_ref[:, i * HD : (i + 1) * HD]
                out_vm[:, (i * G + j) * HD : (i * G + j + 1) * HD] = o.astype(jnp.bfloat16)
            span = pl.ds(i * G * HD, G * HD)
            outs.append(
                pltpu.make_async_copy(out_vm.at[:, span], out_hbm.at[:, span], out_sem.at[i])
            )
            outs[-1].start()

    for one in head_copies.values():
        one.wait_send()

    drain(g, True, (np_ - 1,), (0, 1))
    drain(g, True, range(np_), (2,))

    def settle(dz, carry):
        g0 = 2 * (z - dz) + x

        @pl.when((dz > 0) & held(g0))
        def _():
            drain(g0, True, range(np_))

        g1 = 2 * (z - dz) + 1 - x

        @pl.when(need(g1, g))
        def _():
            drain(g1, False, range(np_))

        return carry

    lax.fori_loop(0, last + 1, settle, 0)
    for one in outs:
        one.wait()


def shards(queries, key_tokens, value_tokens, key_scales, value_scales, value_means, doc_lengths, nseq, nh):
    rows, width = queries.shape
    toks = key_tokens.shape[0]
    hk = width // (G * HD)
    cols = hk * HD
    most = nseq * rows * 5 // 8
    window = (most - 1 + rows - 1) // rows
    reach = (window + 1) // 2
    dims = (nseq // 4, nh, rows, hk, toks, reach)
    hbm = pl.BlockSpec(memory_space=pltpu.HBM)
    dma = pltpu.SemaphoreType.DMA
    return pl.pallas_call(
        functools.partial(kernel, dims),
        out_shape=jax.ShapeDtypeStruct((rows, width), jnp.bfloat16),
        in_specs=[hbm] * 7,
        out_specs=pl.BlockSpec(memory_space=pl.ANY),
        scratch_shapes=[
            pltpu.VMEM((nseq, hk, 2 * rows + 16, HD), jnp.bfloat16),
            pltpu.VMEM((rows, width), jnp.bfloat16),
            pltpu.SMEM(doc_lengths.shape, jnp.int32),
            pltpu.VMEM(key_scales.shape, jnp.bfloat16),
            pltpu.VMEM(value_scales.shape, jnp.bfloat16),
            pltpu.VMEM((1, cols), jnp.float32),
            pltpu.VMEM((hk, G * rows, HD), jnp.bfloat16),
            pltpu.VMEM((hk, G * rows, HD), jnp.float32),
            pltpu.VMEM((hk, G * rows, HD), jnp.float32),
            pltpu.VMEM((hk, G * rows, HD), jnp.float32),
            pltpu.VMEM((math.gcd(hk, 2), G * rows, 2 * rows), jnp.float32),
            pltpu.VMEM((math.gcd(hk, 2), G * rows, 2 * rows), jnp.bfloat16),
            pltpu.VMEM((math.gcd(hk, 2), G * rows, HD), jnp.float32),
            pltpu.VMEM((rows, width), jnp.bfloat16),
            pltpu.VMEM((rows, 2 * rows), jnp.float32),
            pltpu.VMEM((rows, HD), jnp.int32),
            dma((7,)),
            dma((hk,)),
            dma((2, hk)),
            dma((2, hk, max(nh - 1, 1))),
            dma((2, hk, max(nh - 1, 1))),
            dma((3, nseq, hk)),
            dma((nseq, hk)),
        ],
        compiler_params=pltpu.CompilerParams(
            collective_id=0, has_side_effects=True, vmem_limit_bytes=62 * 1024 * 1024
        ),
        cost_estimate=pl.CostEstimate(
            flops=4 * rows * width * 2 * rows * (reach + 1),
            bytes_accessed=4 * rows * width,
            transcendentals=0,
        ),
        name="attend",
    )(
        doc_lengths,
        queries,
        key_tokens,
        value_tokens,
        key_scales,
        value_scales,
        value_means.reshape(1, cols),
    )


def solution(mesh):
    in_specs = (
        P("seq", "head"),
        P(("seq", "head"), None),
        P(("seq", "head"), None),
        P("seq", "head"),
        P("seq", "head"),
        P("head"),
        P(),
    )
    body = functools.partial(shards, nseq=mesh.shape["seq"], nh=mesh.shape["head"])
    return jax.shard_map(body, mesh=mesh, in_specs=in_specs, out_specs=P("seq", "head"), check_vma=False)
```
